128 devices in a mesh: sec: 32 (over y, x_lo, z), strip: 4 (over x_hi, core).
Axes of the slice: x: 4 (x_hi: 2, x_lo: 2; x = x_hi * 2 + x_lo), y: 4, z: 4, core: 2. Of those that a mesh axis runs over, the one named last changes fastest.
Arguments:
- images: bfloat16 [32, 2048, 2048], P('sec', 'strip'), may hold values from -8 to 8
- offsets: int32 [25, 2], replicated, may hold values from -3 to 3, as said below
- springs: int32 [2, 32, 512, 512], P(None, 'sec', 'strip'), may hold values from 1 to 8
- validity: int32 [32, 512, 512], P('sec', 'strip'), may hold values 0 or 1
Outputs:
- relaxed: float32 [2, 32, 512, 512], P(None, 'sec', 'strip')
The draws below stay inside these ranges and needn't reach their ends.
Inputs may be any that keep to these rules, and one draw needn't show every extreme that they name: `offsets`: 25 distinct displacements; among them (0, 0), (-3, -3) and (3, 3).
All inputs are finite; a program needn't handle non-finite values. No bound on the sum of `validity` on one device may be relied on, other than what follows from the above.
Results may differ from the reference program's by a relative error of at most 0.0015.
Values may be sent and summed in bfloat16 or wider, within the bound.
A program may use at most 128 MiB of HBM per device.

```python
import jax
import jax.numpy as jnp
import numpy as np
from jax import lax

WIDTH = 2048
RAD = 3
NOFF = 25
ITERS = 8
SECTIONS = 32
HEIGHT = 2048
NODE_ROWS = 512
NODE_COLS = 512


def draw_images(key, part):
    full_shape = (SECTIONS, HEIGHT, WIDTH)
    own_key = jax.random.fold_in(jax.random.fold_in(key, 11), 0)
    own_part = jax.random.normal(own_key, full_shape, jnp.float32)
    return jnp.clip(own_part, -6.0, 6.0).astype(jnp.bfloat16)


def draw_offsets(key, part):
    extent = 2 * RAD + 1
    cells = extent * extent
    anchors = [cells // 2, 0, cells - 1]
    remaining = np.array([entry for entry in range(cells) if entry not in anchors], dtype=np.int32)
    chosen = jax.random.permutation(jax.random.fold_in(key, 23), remaining.shape[0])[:NOFF - 3]
    selected = jnp.concatenate([jnp.array(anchors, jnp.int32), jnp.asarray(remaining)[chosen]])
    return jnp.stack([selected // extent - RAD, selected % extent - RAD], axis=1).astype(jnp.int32)


def place_ends(values, rng, least, high):
    dims = values.shape
    index_at = [jax.random.randint(jax.random.fold_in(rng, axis), (), 0, dims[axis]) for axis in range(len(dims))]
    values = values.at[tuple(index_at)].set(least)
    longest = dims.index(max(dims))
    index_at[longest] = (index_at[longest] + 1) % dims[longest]
    return values.at[tuple(index_at)].set(high)


def setup_inputs(seed: int = 0) -> dict:
    key_of = jax.random.split(jax.random.key(seed), 5)
    images = draw_images(jax.random.fold_in(key_of[4], 71), 0)
    offsets = draw_offsets(jax.random.fold_in(key_of[4], 71), 0)
    springs = place_ends(jax.random.randint(key_of[2], (2, SECTIONS, NODE_ROWS, NODE_COLS), 1, 9), jax.random.fold_in(key_of[2], 1), 1, 8).astype(jnp.int32)
    validity = place_ends((jax.random.randint(key_of[3], (SECTIONS, NODE_ROWS, NODE_COLS), 0, 4) < 3).astype(jnp.int32), jax.random.fold_in(key_of[3], 1), 0, 1)
    return dict(images=images, offsets=offsets, springs=springs, validity=validity)


sharpness = 0.5
relax_rate = 0.8


def section_flow(current, padded, offsets):
    row_count, col_count = current.shape
    current_f = current.astype(jnp.float32)

    def one_offset(offset):
        shifted = lax.dynamic_slice(padded, (RAD + offset[0], RAD + offset[1]), (row_count, col_count)).astype(jnp.float32)
        product = current_f * shifted
        return sharpness * product.reshape(row_count // 4, 4, col_count // 4, 4).sum(axis=(1, 3))

    scores = lax.map(one_offset, offsets)
    highest = jnp.max(scores, axis=0)
    soft_weights = jnp.exp(scores - highest)
    weight_sum = jnp.sum(soft_weights, axis=0)
    shifts = offsets.astype(jnp.float32)
    flow_row = jnp.sum(soft_weights * shifts[:, 0, None, None], axis=0) / weight_sum
    flow_col = jnp.sum(soft_weights * shifts[:, 1, None, None], axis=0) / weight_sum
    return jnp.stack([flow_row, flow_col])


def advance(positions, from_below, from_above, from_right, from_left, row_weight, weight_up, col_weight, weight_left, pull_term, pull_prior, diagonal):
    force = row_weight * (from_below - positions) + weight_up * (from_above - positions)
    force = force + col_weight * (from_right - positions) + weight_left * (from_left - positions)
    force = force + pull_term - pull_prior
    return positions + relax_rate * force / (1.0 + diagonal)


def reference(images, offsets, springs, validity):
    section_count = images.shape[0]
    extended = jnp.concatenate([images, jnp.zeros_like(images[:1])], axis=0)
    extended = jnp.pad(extended, ((0, 0), (RAD, RAD), (RAD, RAD)))

    def per_section(section):
        current = lax.dynamic_index_in_dim(extended, section, 0, keepdims=False)[RAD:-RAD, RAD:-RAD]
        padded = lax.dynamic_index_in_dim(extended, section + 1, 0, keepdims=False)
        return section_flow(current, padded, offsets)

    flows = lax.map(per_section, jnp.arange(section_count, dtype=jnp.int32))
    keep_mask = (jnp.arange(section_count) < section_count - 1).astype(jnp.float32)
    flow_field = jnp.transpose(flows, (1, 0, 2, 3)) * keep_mask[None, :, None, None]
    node_rows, node_cols = flow_field.shape[2], flow_field.shape[3]
    row_keep = (jnp.arange(node_rows) < node_rows - 1).astype(jnp.float32)
    col_keep = (jnp.arange(node_cols) < node_cols - 1).astype(jnp.float32)
    row_weight = 0.25 * springs[0].astype(jnp.float32) * row_keep[None, :, None]
    col_weight = 0.25 * springs[1].astype(jnp.float32) * col_keep[None, None, :]
    match_weight = validity.astype(jnp.float32) * keep_mask[:, None, None]
    weight_up = jnp.pad(row_weight, ((0, 0), (1, 0), (0, 0)))[:, :-1]
    weight_left = jnp.pad(col_weight, ((0, 0), (0, 0), (1, 0)))[:, :, :-1]
    match_prior = jnp.pad(match_weight, ((1, 0), (0, 0), (0, 0)))[:-1]
    diagonal = row_weight + weight_up + col_weight + weight_left + match_weight + match_prior
    positions = jnp.zeros_like(flow_field)
    for iteration in range(ITERS):
        padded = jnp.pad(positions, ((0, 0), (0, 0), (1, 1), (1, 1)))
        following = jnp.pad(positions, ((0, 0), (0, 1), (0, 0), (0, 0)))[:, 1:]
        pull_term = match_weight * (following - positions - flow_field)
        pull_prior = jnp.pad(pull_term, ((0, 0), (1, 0), (0, 0), (0, 0)))[:, :-1]
        positions = advance(positions, padded[:, :, 2:, 1:-1], padded[:, :, :-2, 1:-1], padded[:, :, 1:-1, 2:], padded[:, :, 1:-1, :-2], row_weight, weight_up, col_weight, weight_left, pull_term, pull_prior, diagonal)
    return positions
```

```python
import jax
import jax.numpy as jnp
from jax import lax
from jax.experimental import pallas as pl
from jax.experimental.pallas import tpu as pltpu
from jax.sharding import PartitionSpec as P

RAD = 3
ITERS = 8
SHARPNESS = 0.5
RELAX_RATE = 0.8
NOFF = 25

BF = jnp.bfloat16
F32 = jnp.float32
MESH = pl.DeviceIdType.MESH
HIGH = lax.Precision.HIGHEST

GROUP = 8
PIX = 64
NODES = 16
SPAN = 40
ORDER = (0, 1, 3, 2)


def part_of(e, t):
    n = jnp.where(e < 4, e, 11 - e)
    return jnp.where(t % 2 == 0, n, 7 - n)


def member_of(c, t):
    n = jnp.where(t % 2 == 0, c, 7 - c)
    return jnp.where(n < 4, n, 11 - n)


def iota(shape, dim):
    return lax.broadcasted_iota(jnp.int32, shape, dim)


def kernel(
    off_ref, x_ref, sp_ref, va_ref, out_ref,
    xs, got, ws, wgot, wup_s, wup_r, cur, nxt, tmp, hs, hr, coef, mf, e0s, e0r, rel, zed, ys, yr, rs_, rr_, ret,
    img_ss, img_rs, fwd_ss, fwd_rs, st_ss, st_rs, ms_ss, ms_rs, hl_ss, hl_rs, wu_ss, wu_rs, e0_ss, e0_rs,
    it_ss, it_rs, rt_ss, rt_rs,
):
    sec = lax.axis_index("sec")
    t = lax.axis_index("strip")
    y, e = sec // 8, sec % 8
    c = part_of(e, t)
    g = t * 8 + c

    def row_device(h):
        h = (h + 32) % 32
        tt = h // 8
        return (8 * y + member_of(h % 8, tt), tt)

    peers = [(8 * y + (e + k) % 8, t) for k in range(1, 8)]
    ynext = ((sec + 8) % 32, t)
    yprev = ((sec + 24) % 32, t)
    below = row_device(g + 1)
    above = row_device(g - 1)
    barrier = pltpu.get_barrier_semaphore()
    everyone = peers + [ynext, yprev, below, above]
    for d in everyone:
        pl.semaphore_signal(barrier, inc=1, device_id=d, device_id_type=MESH)

    source = iota((512, 512), 0)
    target = iota((512, 512), 1)
    spread = (source == 4 * (target % 128) + target // 128).astype(F32).astype(BF)

    def arrange(i, _):
        rows = pl.ds(pl.multiple_of(i * 128, 128), 128)
        for q in range(4):
            block = x_ref[0, rows, 512 * q : 512 * q + 512]
            xs[rows, 512 * q : 512 * q + 512] = jnp.dot(block, spread, preferred_element_type=F32).astype(BF)
        return 0

    lax.fori_loop(0, 4, arrange, 0)

    row_ids = iota((128, 512), 0)
    col_ids = iota((128, 512), 1)
    last_strip = lax.axis_size("strip") - 1
    wr_own = jnp.where((row_ids == 127) & (t == last_strip), 0.0, 0.25 * sp_ref[0, 0].astype(F32))
    wc_own = jnp.where(col_ids == 511, 0.0, 0.25 * sp_ref[1, 0].astype(F32))
    m_own = jnp.where(sec == lax.axis_size("sec") - 1, 0.0, va_ref[0].astype(F32))
    ws[0] = wr_own.astype(BF)
    ws[1] = wc_own.astype(BF)
    ws[2] = m_own.astype(BF)

    a = iota((128, 128), 0)
    b = iota((128, 128), 1)
    turn_f = (b == (a % 8) * 16 + a // 8).astype(F32)
    turn = turn_f.astype(BF)
    back = (a == (b % 8) * 16 + b // 8).astype(F32)

    pl.semaphore_wait(barrier, len(everyone))

    sends = []

    def remote(src, dst, ss, rs, dev):
        copy = pltpu.make_async_remote_copy(
            src_ref=src, dst_ref=dst, send_sem=ss, recv_sem=rs, device_id=dev, device_id_type=MESH
        )
        copy.start()
        sends.append(copy)
        return copy

    def image_copy(blk, k):
        other = (e + k) % 8
        oc = part_of(other, t)
        src = xs.at[pl.ds(pl.multiple_of(64 * oc + 16 * blk, 16), 16)]
        return pltpu.make_async_remote_copy(
            src_ref=src, dst_ref=got.at[e, pl.ds(16 * blk, 16)], send_sem=img_ss.at[blk, k],
            recv_sem=img_rs.at[blk, e], device_id=peers[k - 1], device_id_type=MESH,
        )

    def image_from(blk, s):
        return pltpu.make_async_remote_copy(
            src_ref=xs.at[pl.ds(0, 16)], dst_ref=got.at[s, pl.ds(16 * blk, 16)], send_sem=img_ss.at[blk, 0],
            recv_sem=img_rs.at[blk, s], device_id=peers[0], device_id_type=MESH,
        )

    def static_copy(k):
        other = (e + k) % 8
        oc = part_of(other, t)
        return pltpu.make_async_remote_copy(
            src_ref=ws.at[:, pl.ds(pl.multiple_of(16 * oc, 16), 16)], dst_ref=wgot.at[:, e + 1],
            send_sem=st_ss.at[k], recv_sem=st_rs.at[k], device_id=peers[k - 1], device_id_type=MESH,
        )

    started = []
    for n, blk in enumerate(ORDER):
        for k in range(1, 8):
            copy = image_copy(blk, k)
            copy.start()
            started.append(copy)
        if n == 0:
            statics = [static_copy(k) for k in range(1, 8)]
            for copy in statics:
                copy.start()
    got[e] = xs[pl.ds(pl.multiple_of(64 * c, 64), 64)]
    wgot[:, e + 1] = ws[:, pl.ds(pl.multiple_of(16 * c, 16), 16)]

    def forward(blk):
        @pl.when(e != 0)
        def _():
            image_from(blk, 0).wait_recv()

        return remote(got.at[0, pl.ds(16 * blk, 16)], got.at[8, pl.ds(16 * blk, 16)],
                      fwd_ss.at[blk], fwd_rs.at[blk], yprev)

    def arrive(blk):
        for s in range(1, 8):
            @pl.when(e != s)
            def _():
                image_from(blk, s).wait_recv()

    lane = iota((8, 128), 1)

    def expand(row, src_row):
        base = (row + RAD) * SPAN
        right, left = {}, {}
        for q in range(4):
            for w in range(4):
                plane = tmp[pl.ds(src_row, 8), 512 * q + 128 * w : 512 * q + 128 * w + 128]
                nxt[base + 10 * q + w + 3] = plane
                if w > 0:
                    right[q, w] = pltpu.roll(plane, 1, 1)
                if w < 3:
                    left[q, w] = pltpu.roll(plane, 127, 1)
        for q in range(4):
            for w in range(1, 4):
                carry = right[q - 1, w] if q else jnp.zeros((8, 128), F32)
                nxt[base + 10 * q + w - 1] = jnp.where(lane == 0, carry, right[q, w])
            for w in range(3):
                carry = left[q + 1, w] if q < 3 else jnp.zeros((8, 128), F32)
                nxt[base + 10 * q + w + 7] = jnp.where(lane == 127, carry, left[q, w])

    def convert(blk):
        rows = slice(16 * blk, 16 * blk + 16)
        here = jnp.dot(turn, got[0:8, rows].reshape(128, 2048), preferred_element_type=F32)
        for r in range(16):
            for p in range(16):
                cur[(16 * blk + r) * 16 + p] = here[8 * r : 8 * r + 8, 128 * p : 128 * p + 128]
        tmp[...] = jnp.dot(turn, got[1:9, rows].reshape(128, 2048), preferred_element_type=F32)

        def one(r, _):
            expand(16 * blk + r, pl.multiple_of(r * 8, 8))
            return 0

        lax.fori_loop(0, 16, one, 0)

    def score(first, count):
        def one(i, _):
            q4 = i % 4
            row = first + i // 4
            mine = [[cur[((4 * row + q) * 4 + q4) * 4 + w] for w in range(4)] for q in range(4)]
            scores = []
            for k in range(NOFF):
                at = (4 * row + off_ref[k, 0] + RAD) * SPAN + 10 * q4 + off_ref[k, 1] + RAD
                parts = []
                for q in range(4):
                    p = [mine[q][w] * nxt[at + (q * SPAN + w)] for w in range(4)]
                    parts.append((p[0] + p[1]) + (p[2] + p[3]))
                scores.append((parts[0] + parts[1]) + (parts[2] + parts[3]))
            top = scores[0]
            for k in range(1, NOFF):
                top = jnp.maximum(top, scores[k])
            total = jnp.zeros((8, 128), F32)
            down = jnp.zeros((8, 128), F32)
            side = jnp.zeros((8, 128), F32)
            for k in range(NOFF):
                soft = jnp.exp(SHARPNESS * (scores[k] - top))
                total += soft
                down += soft * off_ref[k, 0].astype(F32)
                side += soft * off_ref[k, 1].astype(F32)
            rows = pl.ds(pl.multiple_of(row * 8, 8), 8)
            match = coef[7, rows, pl.ds(pl.multiple_of(q4 * 128, 128), 128)]
            scale = match / total
            mf[rows, pl.ds(pl.multiple_of(q4 * 128, 128), 128)] = down * scale
            mf[rows, pl.ds(pl.multiple_of(512 + q4 * 128, 128), 128)] = side * scale
            return 0

        lax.fori_loop(0, 4 * count, one, 0)

    forwards = {}
    forwards[0] = forward(0)
    arrive(0)
    for copy in statics:
        copy.wait_recv()
    match_copy = remote(wgot.at[2, 8], wgot.at[2, 0], ms_ss, ms_rs, ynext)
    wr = jnp.dot(turn, wgot[0, 1:9].reshape(128, 512), preferred_element_type=F32)
    wup_s[...] = jnp.concatenate([wr[120:128], wr[120:128]], axis=0).astype(BF)
    up_copy = remote(wup_s, wup_r, wu_ss, wu_rs, below)
    wc = jnp.dot(turn, wgot[1, 1:9].reshape(128, 512), preferred_element_type=F32)
    m = jnp.dot(turn, wgot[2, 1:9].reshape(128, 512), preferred_element_type=F32)
    coef[0] = wr
    coef[2] = wc
    coef[7] = m

    forwards[0].wait_recv()
    convert(0)
    hs[0] = tmp[0:32].astype(BF)
    halo_up = remote(hs.at[0], hr.at[1], hl_ss.at[0], hl_rs.at[0], above)
    forwards[1] = forward(1)
    arrive(1)
    match_copy.wait_recv()
    up_copy.wait_recv()
    wr = coef[0]
    wc = coef[2]
    m = coef[7]
    mp = jnp.dot(turn, wgot[2, 0:8].reshape(128, 512), preferred_element_type=F32)
    wu = jnp.concatenate([wup_r[...].astype(F32)[0:8], wr[0:120]], axis=0)
    wl = jnp.where(col_ids == 0, 0.0, pltpu.roll(wc, 1, 1))
    diagonal = wr + wu + wc + wl + m + mp
    step = RELAX_RATE / (1.0 + diagonal)
    coef[0] = step * wr
    coef[1] = step * wu
    coef[2] = step * wc
    coef[3] = step * wl
    coef[4] = step * m
    coef[5] = step * mp
    coef[6] = 1.0 - step * diagonal
    coef[8] = step

    forwards[1].wait_recv()
    convert(1)
    forwards[3] = forward(3)
    score(1, 6)
    arrive(3)
    forwards[3].wait_recv()
    convert(3)
    hs[1] = tmp[96:128].astype(BF)
    halo_down = remote(hs.at[1], hr.at[0], hl_ss.at[1], hl_rs.at[1], below)
    forwards[2] = forward(2)
    score(13, 2)
    arrive(2)
    forwards[2].wait_recv()
    convert(2)
    score(7, 6)
    halo_up.wait_recv()
    halo_down.wait_recv()
    tmp[0:32] = jnp.where(g == 0, 0.0, hr[0].astype(F32))
    tmp[32:64] = jnp.where(g == 31, 0.0, hr[1].astype(F32))

    def head(r, _):
        expand(r - 3, pl.multiple_of(r * 8 + 8, 8))
        return 0

    lax.fori_loop(0, 3, head, 0)

    def foot(r, _):
        expand(PIX + r, pl.multiple_of(r * 8 + 32, 8))
        return 0

    lax.fori_loop(0, 3, foot, 0)
    score(0, 1)
    score(15, 1)

    u = iota((32, 128), 0)
    v = iota((32, 128), 1)
    pick_f = (v == jnp.where(u < 16, u * 8 + 7, (u - 16) * 8)).astype(F32)
    pick = pick_f.astype(BF)
    u = iota((128, 32), 1)
    v = iota((128, 32), 0)
    put_f = (v == jnp.where(u < 16, u * 8, (u - 16) * 8 + 7)).astype(F32)
    put = put_f.astype(BF)
    e0s[...] = jnp.dot(pick_f[0:16], mf[...], precision=HIGH, preferred_element_type=F32)
    e0 = remote(e0s, e0r, e0_ss, e0_rs, ynext)
    e0.wait_recv()
    zed[...] = jnp.dot(put_f[:, 0:16], e0r[...], precision=HIGH, preferred_element_type=F32)
    sub = iota((8, 512), 0)

    def begin(i, _):
        rows = pl.ds(pl.multiple_of(i * 8, 8), 8)
        for h in range(2):
            cols = slice(512 * h, 512 * h + 512)
            own = mf[rows, cols]
            before = jnp.where(sub == 0, zed[rows, cols], pltpu.roll(own, 1, 0))
            pushed = coef[8, rows] * (before - own)
            mf[rows, cols] = pushed
            rel[0, pl.ds(pl.multiple_of(i * 8 + 8, 8), 8), cols] = pushed
        return 0

    lax.fori_loop(0, NODES, begin, 0)

    def relax(n, _):
        old = n % 2
        new = 1 - old
        body = rel[old, 8:136]
        ys[n] = jnp.dot(pick, body.astype(BF), preferred_element_type=F32).astype(BF)
        rs_[n, 0] = jnp.concatenate([body[0:8, 0:512], body[0:8, 512:1024]], axis=0).astype(BF)
        rs_[n, 1] = jnp.concatenate([body[120:128, 0:512], body[120:128, 512:1024]], axis=0).astype(BF)
        copies = []
        for j, (src, dst, dev) in enumerate((
            (ys.at[n, pl.ds(0, 16)], yr.at[n, pl.ds(0, 16)], ynext),
            (ys.at[n, pl.ds(16, 16)], yr.at[n, pl.ds(16, 16)], yprev),
            (rs_.at[n, 0], rr_.at[n, 0], above),
            (rs_.at[n, 1], rr_.at[n, 1], below),
        )):
            copy = pltpu.make_async_remote_copy(
                src_ref=src, dst_ref=dst, send_sem=it_ss.at[n, j], recv_sem=it_rs.at[n, j],
                device_id=dev, device_id_type=MESH,
            )
            copy.start()
            copies.append(copy)
        for copy in copies:
            copy.wait()
        zed[...] = jnp.dot(put, yr[n], preferred_element_type=F32)
        low = rr_[n, 0].astype(F32)
        high = rr_[n, 1].astype(F32)
        rel[old, 136:144, 0:512] = low[0:8]
        rel[old, 136:144, 512:1024] = low[8:16]
        rel[old, 0:8, 0:512] = high[0:8]
        rel[old, 0:8, 512:1024] = high[8:16]

        def one(i, _):
            rows = pl.ds(pl.multiple_of(i * 8, 8), 8)
            mid = pl.ds(pl.multiple_of(i * 8 + 8, 8), 8)
            far = pl.ds(pl.multiple_of(i * 8 + 16, 8), 8)
            cs = [coef[k, rows] for k in range(7)]
            for h in range(2):
                cols = slice(512 * h, 512 * h + 512)
                own = rel[old, mid, cols]
                edge = zed[rows, cols]
                acc = mf[rows, cols] + cs[6] * own
                acc += cs[0] * rel[old, far, cols] + cs[1] * rel[old, rows, cols]
                acc += cs[2] * pltpu.roll(own, 511, 1) + cs[3] * pltpu.roll(own, 1, 1)
                acc += cs[4] * jnp.where(sub == 7, edge, pltpu.roll(own, 7, 0))
                acc += cs[5] * jnp.where(sub == 0, edge, pltpu.roll(own, 1, 0))
                rel[new, mid, cols] = acc
            return 0

        lax.fori_loop(0, NODES, one, 0)
        return 0

    lax.fori_loop(0, ITERS - 1, relax, 0)

    final = jnp.dot(back, rel[(ITERS - 1) % 2, 8:136], precision=HIGH, preferred_element_type=F32)
    ret[0] = final[:, 0:512]
    ret[1] = final[:, 512:1024]
    place = pl.ds(pl.multiple_of(16 * c, 16), 16)
    returns = []
    for k in range(1, 8):
        other = (e + k) % 8
        copy = pltpu.make_async_remote_copy(
            src_ref=ret.at[:, pl.ds(pl.multiple_of(16 * other, 16), 16)], dst_ref=out_ref.at[:, 0, place],
            send_sem=rt_ss.at[k], recv_sem=rt_rs.at[k], device_id=peers[k - 1], device_id_type=MESH,
        )
        copy.start()
        returns.append(copy)
    out_ref[:, 0, place] = ret[:, pl.ds(pl.multiple_of(16 * e, 16), 16)]
    for k in range(1, 8):
        oc = part_of((e + 8 - k) % 8, t)
        pltpu.make_async_remote_copy(
            src_ref=ret.at[:, pl.ds(0, 16)], dst_ref=out_ref.at[:, 0, pl.ds(pl.multiple_of(16 * oc, 16), 16)],
            send_sem=rt_ss.at[k], recv_sem=rt_rs.at[k], device_id=peers[k - 1], device_id_type=MESH,
        ).wait_recv()
    for copy in returns + started + statics + sends:
        copy.wait_send()


def shards(images, offsets, springs, validity):
    dma = pltpu.SemaphoreType.DMA
    vm = pltpu.VMEM
    whole = pl.BlockSpec(memory_space=pltpu.VMEM)
    return pl.pallas_call(
        kernel,
        out_shape=jax.ShapeDtypeStruct((2, 1, 128, 512), F32),
        in_specs=[pl.BlockSpec(memory_space=pltpu.SMEM), whole, whole, whole],
        out_specs=whole,
        scratch_shapes=[
            vm((512, 2048), BF),
            vm((9, PIX, 2048), BF),
            vm((3, 128, 512), BF),
            vm((3, 9, NODES, 512), BF),
            vm((16, 512), BF),
            vm((16, 512), BF),
            vm((PIX * 16, 8, 128), F32),
            vm(((PIX + 2 * RAD) * SPAN, 8, 128), F32),
            vm((128, 2048), F32),
            vm((2, 32, 2048), BF),
            vm((2, 32, 2048), BF),
            vm((9, 128, 512), F32),
            vm((128, 1024), F32),
            vm((16, 1024), F32),
            vm((16, 1024), F32),
            vm((2, 144, 1024), F32),
            vm((128, 1024), F32),
            vm((ITERS - 1, 32, 1024), BF),
            vm((ITERS - 1, 32, 1024), BF),
            vm((ITERS - 1, 2, 16, 512), BF),
            vm((ITERS - 1, 2, 16, 512), BF),
            vm((2, 128, 512), F32),
            dma((4, 8)), dma((4, 8)), dma((4,)), dma((4,)), dma((8,)), dma((8,)), dma, dma,
            dma((2,)), dma((2,)), dma, dma, dma, dma,
            dma((ITERS - 1, 4)), dma((ITERS - 1, 4)), dma((8,)), dma((8,)),
        ],
        compiler_params=pltpu.CompilerParams(
            collective_id=0, has_side_effects=True, vmem_limit_bytes=48 * 1024 * 1024
        ),
    )(offsets, images, springs, validity)


def solution(mesh):
    in_specs = (
        P("sec", "strip", None),
        P(),
        P(None, "sec", "strip", None),
        P("sec", "strip", None),
    )
    out_specs = P(None, "sec", "strip", None)
    return jax.shard_map(shards, mesh=mesh, in_specs=in_specs, out_specs=out_specs, check_vma=False)
```

```python
import jax
import jax.numpy as jnp
from jax import lax
from jax.experimental import pallas as pl
from jax.experimental.pallas import tpu as pltpu
from jax.sharding import PartitionSpec as P

RAD = 3
ITERS = 8
SHARPNESS = 0.5
RELAX_RATE = 0.8
NOFF = 25

BF = jnp.bfloat16
F32 = jnp.float32
MESH = pl.DeviceIdType.MESH

GROUP = 8
PIX = 64
NODES = 16
SPAN = 40
ORDER = (0, 1, 3, 2)


def part_of(e, t):
    n = jnp.where(e < 4, e, 11 - e)
    return jnp.where(t % 2 == 0, n, 7 - n)


def member_of(c, t):
    n = jnp.where(t % 2 == 0, c, 7 - c)
    return jnp.where(n < 4, n, 11 - n)


def load(ref, rows, first=0):
    return jnp.concatenate([ref[first + q, rows, :] for q in range(4)], axis=1)


def store(ref, rows, value, first=0):
    for q in range(4):
        ref[first + q, rows, :] = value[:, 128 * q : 128 * q + 128]


def iota(shape, dim):
    return lax.broadcasted_iota(jnp.int32, shape, dim)


def kernel(
    off_hbm, x_hbm, sp_hbm, va_hbm, out_ref,
    off_ref, x_ref, sp_ref, va_ref, xs, got, ws, wgot, wup_s, wup_r, cur, nxt, tmp, hs, hr, coef, cn7, cp0, mf, e0s, e0r, rel, ys, yr, rs_, rr_, ret,
    img_ss, img_rs, fwd_ss, fwd_rs, st_ss, st_rs, ms_ss, ms_rs, hl_ss, hl_rs, wu_ss, wu_rs, e0_ss, e0_rs,
    it_ss, it_rs, rt_ss, rt_rs, in_sem,
):
    sec = lax.axis_index("sec")
    t = lax.axis_index("strip")
    y, e = sec // 8, sec % 8
    c = part_of(e, t)
    g = t * 8 + c

    def row_device(h):
        h = (h + 32) % 32
        tt = h // 8
        return (8 * y + member_of(h % 8, tt), tt)

    peers = [(8 * y + (e + k) % 8, t) for k in range(1, 8)]
    ynext = ((sec + 8) % 32, t)
    yprev = ((sec + 24) % 32, t)
    below = row_device(g + 1)
    above = row_device(g - 1)
    barrier = pltpu.get_barrier_semaphore()
    everyone = peers + [ynext, yprev, below, above]
    for d in everyone:
        pl.semaphore_signal(barrier, inc=1, device_id=d, device_id_type=MESH)

    chunks = []
    for i in range(4):
        rows = pl.ds(128 * i, 128)
        chunks.append(pltpu.make_async_copy(x_hbm.at[0, rows], x_ref.at[rows], in_sem.at[i]))
    others = [
        pltpu.make_async_copy(sp_hbm.at[:, 0], sp_ref, in_sem.at[4]),
        pltpu.make_async_copy(va_hbm.at[0], va_ref, in_sem.at[5]),
        pltpu.make_async_copy(off_hbm, off_ref, in_sem.at[6]),
    ]
    for copy in chunks + others:
        copy.start()

    source = iota((512, 512), 0)
    target = iota((512, 512), 1)
    spread = (source == 4 * (target % 128) + target // 128).astype(F32).astype(BF)

    for i in range(4):
        chunks[i].wait()
        rows = slice(128 * i, 128 * i + 128)
        for q in range(4):
            cols = slice(512 * q, 512 * q + 512)
            xs[rows, cols] = jnp.dot(x_ref[rows, cols], spread, preferred_element_type=F32).astype(BF)
    for copy in others:
        copy.wait()

    row_ids = iota((128, 512), 0)
    col_ids = iota((128, 512), 1)
    last_strip = lax.axis_size("strip") - 1
    wr_own = jnp.where((row_ids == 127) & (t == last_strip), 0.0, 0.25 * sp_ref[0].astype(F32))
    wc_own = jnp.where(col_ids == 511, 0.0, 0.25 * sp_ref[1].astype(F32))
    m_own = jnp.where(sec == lax.axis_size("sec") - 1, 0.0, va_ref[...].astype(F32))
    ws[0] = wr_own.astype(BF)
    ws[1] = wc_own.astype(BF)
    ws[2] = m_own.astype(BF)

    a = iota((128, 128), 0)
    b = iota((128, 128), 1)
    turn = (b == (a % 8) * 16 + a // 8).astype(F32).astype(BF)

    pl.semaphore_wait(barrier, len(everyone))

    sends = []

    def remote(src, dst, ss, rs, dev):
        copy = pltpu.make_async_remote_copy(
            src_ref=src, dst_ref=dst, send_sem=ss, recv_sem=rs, device_id=dev, device_id_type=MESH
        )
        copy.start()
        sends.append(copy)
        return copy

    def image_copy(blk, k):
        other = (e + k) % 8
        oc = part_of(other, t)
        src = xs.at[pl.ds(pl.multiple_of(64 * oc + 16 * blk, 16), 16)]
        return pltpu.make_async_remote_copy(
            src_ref=src, dst_ref=got.at[e, pl.ds(16 * blk, 16)], send_sem=img_ss.at[blk, k],
            recv_sem=img_rs.at[blk, e], device_id=peers[k - 1], device_id_type=MESH,
        )

    def image_from(blk, s):
        return pltpu.make_async_remote_copy(
            src_ref=xs.at[pl.ds(0, 16)], dst_ref=got.at[s, pl.ds(16 * blk, 16)], send_sem=img_ss.at[blk, 0],
            recv_sem=img_rs.at[blk, s], device_id=peers[0], device_id_type=MESH,
        )

    def static_copy(k):
        other = (e + k) % 8
        oc = part_of(other, t)
        return pltpu.make_async_remote_copy(
            src_ref=ws.at[:, pl.ds(pl.multiple_of(16 * oc, 16), 16)], dst_ref=wgot.at[:, e + 1],
            send_sem=st_ss.at[k], recv_sem=st_rs.at[k], device_id=peers[k - 1], device_id_type=MESH,
        )

    started = []
    for blk in ORDER:
        for k in range(1, 8):
            copy = image_copy(blk, k)
            copy.start()
            started.append(copy)
    statics = [static_copy(k) for k in range(1, 8)]
    for copy in statics:
        copy.start()
    got[e] = xs[pl.ds(pl.multiple_of(64 * c, 64), 64)]
    wgot[:, e + 1] = ws[:, pl.ds(pl.multiple_of(16 * c, 16), 16)]

    def forward(blk):
        @pl.when(e != 0)
        def _():
            image_from(blk, 0).wait_recv()

        return remote(got.at[0, pl.ds(16 * blk, 16)], got.at[8, pl.ds(16 * blk, 16)],
                      fwd_ss.at[blk], fwd_rs.at[blk], yprev)

    def arrive(blk):
        for s in range(1, 8):
            @pl.when(e != s)
            def _():
                image_from(blk, s).wait_recv()

    lane = iota((8, 128), 1)

    def expand(row, src_row):
        base = (row + RAD) * SPAN
        right, left = {}, {}
        for q in range(4):
            for w in range(4):
                plane = tmp[pl.ds(src_row, 8), 512 * q + 128 * w : 512 * q + 128 * w + 128]
                nxt[base + 10 * q + w + 3] = plane
                if w > 0:
                    right[q, w] = pltpu.roll(plane, 1, 1)
                if w < 3:
                    left[q, w] = pltpu.roll(plane, 127, 1)
        for q in range(4):
            for w in range(1, 4):
                carry = right[q - 1, w] if q else jnp.zeros((8, 128), F32)
                nxt[base + 10 * q + w - 1] = jnp.where(lane == 0, carry, right[q, w])
            for w in range(3):
                carry = left[q + 1, w] if q < 3 else jnp.zeros((8, 128), F32)
                nxt[base + 10 * q + w + 7] = jnp.where(lane == 127, carry, left[q, w])

    def convert(blk):
        rows = slice(16 * blk, 16 * blk + 16)
        here = jnp.dot(turn, got[0:8, rows].reshape(128, 2048), preferred_element_type=F32)
        for r in range(16):
            for p in range(16):
                cur[(16 * blk + r) * 16 + p] = here[8 * r : 8 * r + 8, 128 * p : 128 * p + 128]
        tmp[...] = jnp.dot(turn, got[1:9, rows].reshape(128, 2048), preferred_element_type=F32)

        def one(r, _):
            expand(16 * blk + r, pl.multiple_of(r * 8, 8))
            return 0

        lax.fori_loop(0, 16, one, 0)

    def score(first, count):
        def one(i, _):
            q4 = i % 4
            row = first + i // 4
            mine = [[cur[((4 * row + q) * 4 + q4) * 4 + w] for w in range(4)] for q in range(4)]
            scores = []
            for k in range(NOFF):
                at = (4 * row + off_ref[k, 0] + RAD) * SPAN + 10 * q4 + off_ref[k, 1] + RAD
                parts = []
                for q in range(4):
                    p = [mine[q][w] * nxt[at + (q * SPAN + w)] for w in range(4)]
                    parts.append((p[0] + p[1]) + (p[2] + p[3]))
                scores.append((parts[0] + parts[1]) + (parts[2] + parts[3]))
            top = scores[0]
            for k in range(1, NOFF):
                top = jnp.maximum(top, scores[k])
            total = jnp.zeros((8, 128), F32)
            down = jnp.zeros((8, 128), F32)
            side = jnp.zeros((8, 128), F32)
            for k in range(NOFF):
                soft = jnp.exp(SHARPNESS * (scores[k] - top))
                total += soft
                down += soft * off_ref[k, 0].astype(F32)
                side += soft * off_ref[k, 1].astype(F32)
            rows = pl.ds(pl.multiple_of(row * 8, 8), 8)
            scale = 1.0 / total
            mf[q4, rows] = down * scale
            mf[4 + q4, rows] = side * scale
            return 0

        lax.fori_loop(0, 4 * count, one, 0)

    forward_0 = forward(0)
    arrive(0)
    forward_0.wait_recv()
    convert(0)
    hs[0] = tmp[0:32].astype(BF)
    halo_up = remote(hs.at[0], hr.at[1], hl_ss.at[0], hl_rs.at[0], above)
    forward_1 = forward(1)
    arrive(1)
    forward_1.wait_recv()
    convert(1)
    forward_3 = forward(3)
    score(1, 6)
    arrive(3)
    forward_3.wait_recv()
    convert(3)
    hs[1] = tmp[96:128].astype(BF)
    halo_down = remote(hs.at[1], hr.at[0], hl_ss.at[1], hl_rs.at[1], below)
    forward_2 = forward(2)
    score(13, 2)
    halo_up.wait_recv()
    halo_down.wait_recv()
    tmp[0:32] = jnp.where(g == 0, 0.0, hr[0].astype(F32))
    tmp[32:64] = jnp.where(g == 31, 0.0, hr[1].astype(F32))

    def head(r, _):
        expand(r - 3, pl.multiple_of(r * 8 + 8, 8))
        return 0

    lax.fori_loop(0, 3, head, 0)

    def foot(r, _):
        expand(PIX + r, pl.multiple_of(r * 8 + 32, 8))
        return 0

    lax.fori_loop(0, 3, foot, 0)
    score(0, 1)
    score(15, 1)
    arrive(2)
    forward_2.wait_recv()
    convert(2)

    for copy in statics:
        copy.wait_recv()
    match_copy = remote(wgot.at[2, 8], wgot.at[2, 0], ms_ss, ms_rs, ynext)
    every = slice(0, 128)
    wr = jnp.dot(turn, wgot[0, 1:9].reshape(128, 512), preferred_element_type=F32)
    wup_s[...] = jnp.concatenate([wr[120:128], wr[120:128]], axis=0).astype(BF)
    up_copy = remote(wup_s, wup_r, wu_ss, wu_rs, below)
    store(coef.at[0], every, wr)
    store(coef.at[2], every, jnp.dot(turn, wgot[1, 1:9].reshape(128, 512), preferred_element_type=F32))
    store(coef.at[7], every, jnp.dot(turn, wgot[2, 1:9].reshape(128, 512), preferred_element_type=F32))

    score(7, 6)

    def strided(s, start=0):
        return pl.ds(start + s, NODES, stride=8)

    for p in range(8):
        e0s[:, 128 * p : 128 * p + 128] = mf[p, strided(7), :] * coef[7, p % 4, strided(7), :]
    e0 = remote(e0s, e0r, e0_ss, e0_rs, ynext)

    match_copy.wait_recv()
    up_copy.wait_recv()
    store(coef.at[5], every, jnp.dot(turn, wgot[2, 0:8].reshape(128, 512), preferred_element_type=F32))
    sub = iota((8, 512), 0)
    col = iota((8, 512), 1)
    for p in range(8):
        for o in range(2):
            rel[o, p, 0:8] = jnp.zeros((8, 128), F32)
            rel[o, p, 136:144] = jnp.zeros((8, 128), F32)
    wu_next = wup_r[...].astype(F32)[0:8]
    for i in range(NODES):
        rows = slice(8 * i, 8 * i + 8)
        wu = wu_next
        wr = load(coef.at[0], rows)
        wu_next = wr
        wc = load(coef.at[2], rows)
        m = load(coef.at[7], rows)
        mp = load(coef.at[5], rows)
        wl = jnp.where(col == 0, 0.0, pltpu.roll(wc, 1, 1))
        diagonal = wr + wu + wc + wl + m + mp
        step = RELAX_RATE / (1.0 + diagonal)
        for k, factor in enumerate((wr, wu, wc, wl, m, mp)):
            store(coef.at[k], rows, step * factor)
        store(coef.at[6], rows, 1.0 - step * diagonal)
        store(coef.at[7], rows, step)
        for h in range(2):
            own = m * load(mf, rows, 4 * h)
            pushed = step * (jnp.where(sub == 0, 0.0, pltpu.roll(own, 1, 0)) - own)
            store(mf, rows, pushed, 4 * h)
    for p in range(8):
        cn7[p] = coef[4, p % 4, strided(7), :]
        cp0[p] = coef[5, p % 4, strided(0), :]
    e0.wait_recv()
    for p in range(8):
        step0 = coef[7, p % 4, strided(0), :]
        mf[p, strided(0), :] = mf[p, strided(0), :] + step0 * e0r[:, 128 * p : 128 * p + 128]
    for p in range(8):
        rel[0, p, 8:136] = mf[p]

    def relax(n, _):
        old = n % 2
        new = 1 - old
        for p in range(8):
            ys[n, 0:16, 128 * p : 128 * p + 128] = rel[old, p, strided(7, 8), :].astype(BF)
            ys[n, 16:32, 128 * p : 128 * p + 128] = rel[old, p, strided(0, 8), :].astype(BF)
        for j, rows in enumerate((slice(8, 16), slice(128, 136))):
            ends = [load(rel.at[old], rows, 4 * h) for h in range(2)]
            rs_[n, j] = jnp.concatenate(ends, axis=0).astype(BF)
        copies = []
        for j, (src, dst, dev) in enumerate((
            (ys.at[n, pl.ds(0, 16)], yr.at[n, pl.ds(0, 16)], ynext),
            (ys.at[n, pl.ds(16, 16)], yr.at[n, pl.ds(16, 16)], yprev),
            (rs_.at[n, 0], rr_.at[n, 0], above),
            (rs_.at[n, 1], rr_.at[n, 1], below),
        )):
            copy = pltpu.make_async_remote_copy(
                src_ref=src, dst_ref=dst, send_sem=it_ss.at[n, j], recv_sem=it_rs.at[n, j],
                device_id=dev, device_id_type=MESH,
            )
            copy.start()
            copies.append(copy)

        def some(i4, _):
            for i in range(4):
                start = pl.multiple_of(i4 * 32, 32)
                rows = pl.ds(pl.multiple_of(start + 8 * i, 8), 8)
                mid = pl.ds(pl.multiple_of(start + 8 * i + 8, 8), 8)
                far = pl.ds(pl.multiple_of(start + 8 * i + 16, 8), 8)
                cs = [load(coef.at[k], rows) for k in range(7)]
                inner_n = jnp.where(sub == 7, 0.0, cs[4])
                inner_p = jnp.where(sub == 0, 0.0, cs[5])
                for h in range(2):
                    own = load(rel.at[old], mid, 4 * h)
                    acc = load(mf, rows, 4 * h) + cs[6] * own
                    acc += cs[0] * load(rel.at[old], far, 4 * h) + cs[1] * load(rel.at[old], rows, 4 * h)
                    acc += cs[2] * pltpu.roll(own, 511, 1) + cs[3] * pltpu.roll(own, 1, 1)
                    acc += inner_n * pltpu.roll(own, 7, 0) + inner_p * pltpu.roll(own, 1, 0)
                    store(rel.at[new], mid, acc, 4 * h)
            return 0

        lax.fori_loop(0, NODES // 4, some, 0)
        copies[2].wait()
        copies[3].wait()
        high = rr_[n, 1].astype(F32)
        low = rr_[n, 0].astype(F32)
        for p in range(8):
            part = slice(8 * (p // 4), 8 * (p // 4) + 8)
            cols = slice(128 * (p % 4), 128 * (p % 4) + 128)
            rel[new, p, 128:136] = rel[new, p, 128:136] + coef[0, p % 4, 120:128] * low[part, cols]
            rel[new, p, 8:16] = rel[new, p, 8:16] + coef[1, p % 4, 0:8] * high[part, cols]
        copies[0].wait()
        copies[1].wait()
        for p in range(8):
            cols = slice(128 * p, 128 * p + 128)
            edge = rel[new, p, strided(0, 8), :] + cp0[p] * yr[n, 0:16, cols].astype(F32)
            rel[new, p, strided(0, 8), :] = edge
            edge = rel[new, p, strided(7, 8), :] + cn7[p] * yr[n, 16:32, cols].astype(F32)
            rel[new, p, strided(7, 8), :] = edge
        return 0

    lax.fori_loop(0, ITERS - 1, relax, 0)

    done = (ITERS - 1) % 2
    for s in range(8):
        for p in range(8):
            cols = slice(128 * (p % 4), 128 * (p % 4) + 128)
            ret[p // 4, 16 * s : 16 * s + 16, cols] = rel[done, p, strided(s, 8), :]
    place = pl.ds(pl.multiple_of(16 * c, 16), 16)
    returns = []
    for k in range(1, 8):
        other = (e + k) % 8
        copy = pltpu.make_async_remote_copy(
            src_ref=ret.at[:, pl.ds(pl.multiple_of(16 * other, 16), 16)], dst_ref=out_ref.at[:, 0, place],
            send_sem=rt_ss.at[k], recv_sem=rt_rs.at[k], device_id=peers[k - 1], device_id_type=MESH,
        )
        copy.start()
        returns.append(copy)
    out_ref[:, 0, place] = ret[:, pl.ds(pl.multiple_of(16 * e, 16), 16)]
    for k in range(1, 8):
        oc = part_of((e + 8 - k) % 8, t)
        pltpu.make_async_remote_copy(
            src_ref=ret.at[:, pl.ds(0, 16)], dst_ref=out_ref.at[:, 0, pl.ds(pl.multiple_of(16 * oc, 16), 16)],
            send_sem=rt_ss.at[k], recv_sem=rt_rs.at[k], device_id=peers[k - 1], device_id_type=MESH,
        ).wait_recv()
    for copy in returns + started + statics + sends:
        copy.wait_send()


def shards(images, offsets, springs, validity):
    dma = pltpu.SemaphoreType.DMA
    vm = pltpu.VMEM
    whole = pl.BlockSpec(memory_space=pltpu.VMEM)
    return pl.pallas_call(
        kernel,
        out_shape=jax.ShapeDtypeStruct((2, 1, 128, 512), F32),
        in_specs=[pl.BlockSpec(memory_space=pltpu.HBM)] * 4,
        out_specs=whole,
        scratch_shapes=[
            pltpu.SMEM((NOFF, 2), jnp.int32),
            vm((512, 2048), BF),
            vm((2, 128, 512), jnp.int32),
            vm((128, 512), jnp.int32),
            vm((512, 2048), BF),
            vm((9, PIX, 2048), BF),
            vm((3, 128, 512), BF),
            vm((3, 9, NODES, 512), BF),
            vm((16, 512), BF),
            vm((16, 512), BF),
            vm((PIX * 16, 8, 128), F32),
            vm(((PIX + 2 * RAD) * SPAN, 8, 128), F32),
            vm((128, 2048), F32),
            vm((2, 32, 2048), BF),
            vm((2, 32, 2048), BF),
            vm((8, 4, 128, 128), F32),
            vm((8, 16, 128), F32),
            vm((8, 16, 128), F32),
            vm((8, 128, 128), F32),
            vm((16, 1024), F32),
            vm((16, 1024), F32),
            vm((2, 8, 144, 128), F32),
            vm((ITERS - 1, 32, 1024), BF),
            vm((ITERS - 1, 32, 1024), BF),
            vm((ITERS - 1, 2, 16, 512), BF),
            vm((ITERS - 1, 2, 16, 512), BF),
            vm((2, 128, 512), F32),
            dma((4, 8)), dma((4, 8)), dma((4,)), dma((4,)), dma((8,)), dma((8,)), dma, dma,
            dma((2,)), dma((2,)), dma, dma, dma, dma,
            dma((ITERS - 1, 4)), dma((ITERS - 1, 4)), dma((8,)), dma((8,)), dma((8,)),
        ],
        compiler_params=pltpu.CompilerParams(
            collective_id=0, has_side_effects=True, vmem_limit_bytes=48 * 1024 * 1024
        ),
    )(offsets, images, springs, validity)


def solution(mesh):
    in_specs = (
        P("sec", "strip", None),
        P(),
        P(None, "sec", "strip", None),
        P("sec", "strip", None),
    )
    out_specs = P(None, "sec", "strip", None)
    return jax.shard_map(shards, mesh=mesh, in_specs=in_specs, out_specs=out_specs, check_vma=False)
```

```python
import jax
import jax.numpy as jnp
from jax import lax
from jax.experimental import pallas as pl
from jax.experimental.pallas import tpu as pltpu
from jax.sharding import PartitionSpec as P

RAD = 3
ITERS = 8
SHARPNESS = 0.5
RELAX_RATE = 0.8
NOFF = 25

BF = jnp.bfloat16
F32 = jnp.float32
MESH = pl.DeviceIdType.MESH

GROUP = 8
PIX = 64
NODES = 16
SPAN = 40
ORDER = (0, 1, 3, 2)


def part_of(e, t):
    n = jnp.where(e < 4, e, 11 - e)
    return jnp.where(t % 2 == 0, n, 7 - n)


def member_of(c, t):
    n = jnp.where(t % 2 == 0, c, 7 - c)
    return jnp.where(n < 4, n, 11 - n)


def load(ref, rows, first=0):
    return jnp.concatenate([ref[first + q, rows, :] for q in range(4)], axis=1)


def store(ref, rows, value, first=0):
    for q in range(4):
        ref[first + q, rows, :] = value[:, 128 * q : 128 * q + 128]


def iota(shape, dim):
    return lax.broadcasted_iota(jnp.int32, shape, dim)


def kernel(
    off_hbm, x_hbm, sp_hbm, va_hbm, early_ref, late_ref,
    off_ref, x_ref, sp_ref, va_ref, xs, got, ws, wgot, wup_s, wup_r, cur, nxt, tmp, hs, hr, coef, cn7, cp0, mf, e0s, e0r, rel, ys, yr, rs_, rr_, ret,
    img_ss, img_rs, fwd_ss, fwd_rs, st_ss, st_rs, ms_ss, ms_rs, hl_ss, hl_rs, wu_ss, wu_rs, e0_ss, e0_rs,
    it_ss, it_rs, rt_ss, rt_rs, in_sem,
):
    sec = lax.axis_index("sec")
    t = lax.axis_index("strip")
    y, e = sec // 8, sec % 8
    c = part_of(e, t)
    g = t * 8 + c

    def row_device(h):
        h = (h + 32) % 32
        tt = h // 8
        return (8 * y + member_of(h % 8, tt), tt)

    peers = [(8 * y + (e + k) % 8, t) for k in range(1, 8)]
    ynext = ((sec + 8) % 32, t)
    yprev = ((sec + 24) % 32, t)
    below = row_device(g + 1)
    above = row_device(g - 1)
    barrier = pltpu.get_barrier_semaphore()
    everyone = peers + [ynext, yprev, below, above]
    for d in everyone:
        pl.semaphore_signal(barrier, inc=1, device_id=d, device_id_type=MESH)

    chunks = []
    for i in range(4):
        rows = pl.ds(128 * i, 128)
        chunks.append(pltpu.make_async_copy(x_hbm.at[0, rows], x_ref.at[rows], in_sem.at[i]))
    others = [
        pltpu.make_async_copy(sp_hbm.at[:, 0], sp_ref, in_sem.at[4]),
        pltpu.make_async_copy(va_hbm.at[0], va_ref, in_sem.at[5]),
        pltpu.make_async_copy(off_hbm, off_ref, in_sem.at[6]),
    ]
    for copy in chunks + others:
        copy.start()

    source = iota((512, 512), 0)
    target = iota((512, 512), 1)
    spread = (source == 4 * (target % 128) + target // 128).astype(F32).astype(BF)

    for i in range(4):
        chunks[i].wait()
        rows = slice(128 * i, 128 * i + 128)
        for q in range(4):
            cols = slice(512 * q, 512 * q + 512)
            xs[rows, cols] = jnp.dot(x_ref[rows, cols], spread, preferred_element_type=F32).astype(BF)
    for copy in others:
        copy.wait()

    row_ids = iota((128, 512), 0)
    col_ids = iota((128, 512), 1)
    last_strip = lax.axis_size("strip") - 1
    wr_own = jnp.where((row_ids == 127) & (t == last_strip), 0.0, 0.25 * sp_ref[0].astype(F32))
    wc_own = jnp.where(col_ids == 511, 0.0, 0.25 * sp_ref[1].astype(F32))
    m_own = jnp.where(sec == lax.axis_size("sec") - 1, 0.0, va_ref[...].astype(F32))
    ws[0] = wr_own.astype(BF)
    ws[1] = wc_own.astype(BF)
    ws[2] = m_own.astype(BF)

    a = iota((128, 128), 0)
    b = iota((128, 128), 1)
    turn = (b == (a % 8) * 16 + a // 8).astype(F32).astype(BF)

    pl.semaphore_wait(barrier, len(everyone))

    sends = []

    def remote(src, dst, ss, rs, dev):
        copy = pltpu.make_async_remote_copy(
            src_ref=src, dst_ref=dst, send_sem=ss, recv_sem=rs, device_id=dev, device_id_type=MESH
        )
        copy.start()
        sends.append(copy)
        return copy

    def image_copy(blk, k):
        other = (e + k) % 8
        oc = part_of(other, t)
        src = xs.at[pl.ds(pl.multiple_of(64 * oc + 16 * blk, 16), 16)]
        return pltpu.make_async_remote_copy(
            src_ref=src, dst_ref=got.at[e, pl.ds(16 * blk, 16)], send_sem=img_ss.at[blk, k],
            recv_sem=img_rs.at[blk, e], device_id=peers[k - 1], device_id_type=MESH,
        )

    def image_from(blk, s):
        return pltpu.make_async_remote_copy(
            src_ref=xs.at[pl.ds(0, 16)], dst_ref=got.at[s, pl.ds(16 * blk, 16)], send_sem=img_ss.at[blk, 0],
            recv_sem=img_rs.at[blk, s], device_id=peers[0], device_id_type=MESH,
        )

    def static_copy(k):
        other = (e + k) % 8
        oc = part_of(other, t)
        return pltpu.make_async_remote_copy(
            src_ref=ws.at[:, pl.ds(pl.multiple_of(16 * oc, 16), 16)], dst_ref=wgot.at[:, e + 1],
            send_sem=st_ss.at[k], recv_sem=st_rs.at[k], device_id=peers[k - 1], device_id_type=MESH,
        )

    started = []
    for blk in ORDER:
        for k in range(1, 8):
            copy = image_copy(blk, k)
            copy.start()
            started.append(copy)
    statics = [static_copy(k) for k in range(1, 8)]
    got[e] = xs[pl.ds(pl.multiple_of(64 * c, 64), 64)]
    wgot[:, e + 1] = ws[:, pl.ds(pl.multiple_of(16 * c, 16), 16)]

    def forward(blk):
        @pl.when(e != 0)
        def _():
            image_from(blk, 0).wait_recv()

        return remote(got.at[0, pl.ds(16 * blk, 16)], got.at[8, pl.ds(16 * blk, 16)],
                      fwd_ss.at[blk], fwd_rs.at[blk], yprev)

    def arrive(blk):
        for s in range(1, 8):
            @pl.when(e != s)
            def _():
                image_from(blk, s).wait_recv()

    lane = iota((8, 128), 1)

    def expand(row, src_row):
        base = (row + RAD) * SPAN
        right, left = {}, {}
        for q in range(4):
            for w in range(4):
                plane = tmp[pl.ds(src_row, 8), 512 * q + 128 * w : 512 * q + 128 * w + 128]
                nxt[base + 10 * q + w + 3] = plane
                if w > 0:
                    right[q, w] = pltpu.roll(plane, 1, 1)
                if w < 3:
                    left[q, w] = pltpu.roll(plane, 127, 1)
        for q in range(4):
            for w in range(1, 4):
                carry = right[q - 1, w] if q else jnp.zeros((8, 128), F32)
                nxt[base + 10 * q + w - 1] = jnp.where(lane == 0, carry, right[q, w])
            for w in range(3):
                carry = left[q + 1, w] if q < 3 else jnp.zeros((8, 128), F32)
                nxt[base + 10 * q + w + 7] = jnp.where(lane == 127, carry, left[q, w])

    def convert_own(blk):
        rows = slice(16 * blk, 16 * blk + 16)
        here = jnp.dot(turn, got[0:8, rows].reshape(128, 2048), preferred_element_type=F32)
        for r in range(16):
            for p in range(16):
                cur[(16 * blk + r) * 16 + p] = here[8 * r : 8 * r + 8, 128 * p : 128 * p + 128]

    def convert(blk):
        rows = slice(16 * blk, 16 * blk + 16)
        tmp[...] = jnp.dot(turn, got[1:9, rows].reshape(128, 2048), preferred_element_type=F32)

        def one(r, _):
            expand(16 * blk + r, pl.multiple_of(r * 8, 8))
            return 0

        lax.fori_loop(0, 16, one, 0)

    def score(first, count):
        def one(i, _):
            q4 = i % 4
            row = first + i // 4
            mine = [[cur[((4 * row + q) * 4 + q4) * 4 + w] for w in range(4)] for q in range(4)]
            scores = []
            for k in range(NOFF):
                at = (4 * row + off_ref[0, k] + RAD) * SPAN + 10 * q4 + off_ref[1, k] + RAD
                parts = []
                for q in range(4):
                    p = [mine[q][w] * nxt[at + (q * SPAN + w)] for w in range(4)]
                    parts.append((p[0] + p[1]) + (p[2] + p[3]))
                scores.append((parts[0] + parts[1]) + (parts[2] + parts[3]))
            top = scores[0]
            for k in range(1, NOFF):
                top = jnp.maximum(top, scores[k])
            total = jnp.zeros((8, 128), F32)
            down = jnp.zeros((8, 128), F32)
            side = jnp.zeros((8, 128), F32)
            for k in range(NOFF):
                soft = jnp.exp(SHARPNESS * (scores[k] - top))
                total += soft
                down += soft * off_ref[0, k].astype(F32)
                side += soft * off_ref[1, k].astype(F32)
            rows = pl.ds(pl.multiple_of(row * 8, 8), 8)
            scale = 1.0 / total
            mf[q4, rows] = down * scale
            mf[4 + q4, rows] = side * scale
            return 0

        lax.fori_loop(0, 4 * count, one, 0)

    def halves(rows):
        return jnp.concatenate([tmp[rows, 0:1024], tmp[rows, 1024:2048]], axis=0).astype(BF)

    def halo(j, row, outside):
        came = jnp.where(outside, 0.0, hr[j].astype(F32))
        tmp[0:24, 0:1024] = came[0:24]
        tmp[0:24, 1024:2048] = came[24:48]

        def one(r, _):
            expand(row + r, pl.multiple_of(r * 8, 8))
            return 0

        lax.fori_loop(0, 3, one, 0)

    every = slice(0, 128)
    forward_0 = forward(0)
    arrive(0)
    convert_own(0)
    forward_0.wait_recv()
    convert(0)
    hs[0] = halves(slice(0, 24))
    forward_1 = forward(1)
    arrive(1)
    convert_own(1)
    forward_1.wait_recv()
    convert(1)
    forward_3 = forward(3)
    score(1, 4)
    arrive(3)
    convert_own(3)
    forward_3.wait_recv()
    convert(3)
    hs[1] = halves(slice(104, 128))
    forward_2 = forward(2)
    for copy in statics:
        copy.start()
    halo_up = remote(hs.at[0], hr.at[1], hl_ss.at[0], hl_rs.at[0], above)
    halo_down = remote(hs.at[1], hr.at[0], hl_ss.at[1], hl_rs.at[1], below)
    score(5, 2)
    arrive(2)
    convert_own(2)
    score(13, 2)
    forward_2.wait_recv()
    convert(2)

    for copy in statics:
        copy.wait_recv()
    match_copy = remote(wgot.at[2, 8], wgot.at[2, 0], ms_ss, ms_rs, ynext)
    wr = jnp.dot(turn, wgot[0, 1:9].reshape(128, 512), preferred_element_type=F32)
    wup_s[...] = jnp.concatenate([wr[120:128], wr[120:128]], axis=0).astype(BF)
    up_copy = remote(wup_s, wup_r, wu_ss, wu_rs, below)
    store(coef.at[0], every, wr)
    store(coef.at[2], every, jnp.dot(turn, wgot[1, 1:9].reshape(128, 512), preferred_element_type=F32))
    store(coef.at[8], every, jnp.dot(turn, wgot[2, 1:9].reshape(128, 512), preferred_element_type=F32))
    score(7, 6)

    match_copy.wait_recv()
    up_copy.wait_recv()
    store(coef.at[5], every, jnp.dot(turn, wgot[2, 0:8].reshape(128, 512), preferred_element_type=F32))
    sub = iota((8, 512), 0)
    col = iota((8, 512), 1)
    for p in range(8):
        for o in range(2):
            rel[o, p, 0:8] = jnp.zeros((8, 128), F32)
            rel[o, p, 136:144] = jnp.zeros((8, 128), F32)
    wu_next = wup_r[...].astype(F32)[0:8]
    for i in range(NODES):
        rows = slice(8 * i, 8 * i + 8)
        wu = wu_next
        wr = load(coef.at[0], rows)
        wu_next = wr
        wc = load(coef.at[2], rows)
        m = load(coef.at[8], rows)
        mp = load(coef.at[5], rows)
        wl = jnp.where(col == 0, 0.0, pltpu.roll(wc, 1, 1))
        diagonal = wr + wu + wc + wl + m + mp
        step = RELAX_RATE / (1.0 + diagonal)
        for k, factor in enumerate((wr, wu, wc, wl, m, mp)):
            store(coef.at[k], rows, step * factor)
        store(coef.at[6], rows, 1.0 - step * diagonal)
        store(coef.at[7], rows, step)

    def strided(s, start=0):
        return pl.ds(start + s, NODES, stride=8)

    for p in range(8):
        cn7[p] = coef[4, p % 4, strided(7), :]
        cp0[p] = coef[5, p % 4, strided(0), :]

    halo_up.wait_recv()
    halo(1, PIX, g == 31)
    halo_down.wait_recv()
    halo(0, -RAD, g == 0)
    score(0, 1)
    score(15, 1)

    for p in range(8):
        e0s[:, 128 * p : 128 * p + 128] = mf[p, strided(7), :] * coef[8, p % 4, strided(7), :]
    e0 = remote(e0s, e0r, e0_ss, e0_rs, ynext)
    for i in range(NODES):
        rows = slice(8 * i, 8 * i + 8)
        m = load(coef.at[8], rows)
        step = load(coef.at[7], rows)
        for h in range(2):
            own = m * load(mf, rows, 4 * h)
            pushed = step * (jnp.where(sub == 0, 0.0, pltpu.roll(own, 1, 0)) - own)
            store(mf, rows, pushed, 4 * h)
            store(rel.at[0], slice(8 * i + 8, 8 * i + 16), pushed, 4 * h)
    e0.wait_recv()
    for p in range(8):
        step0 = coef[7, p % 4, strided(0), :]
        first = mf[p, strided(0), :] + step0 * e0r[:, 128 * p : 128 * p + 128]
        mf[p, strided(0), :] = first
        rel[0, p, strided(0, 8), :] = first

    def send_back(src, dst, half):
        for k in range(1, 8):
            other = (e + k) % 8
            copy = pltpu.make_async_remote_copy(
                src_ref=src.at[:, pl.ds(pl.multiple_of(16 * other, 16), 16)], dst_ref=dst.at[:, 0, place],
                send_sem=rt_ss.at[half, k], recv_sem=rt_rs.at[half, k], device_id=peers[k - 1], device_id_type=MESH,
            )
            copy.start()
            returns.append(copy)
        own = pltpu.make_async_copy(
            src.at[:, pl.ds(pl.multiple_of(16 * e, 16), 16)], dst.at[:, 0, place], rt_ss.at[half, 0]
        )
        own.start()
        owns.append(own)

    returns, owns = [], []
    place = pl.ds(pl.multiple_of(16 * c, 16), 16)

    def relax(n, last):
        old = n % 2
        new = 1 - old
        for p in range(8):
            ys[n, 0:16, 128 * p : 128 * p + 128] = rel[old, p, strided(7, 8), :].astype(BF)
            ys[n, 16:32, 128 * p : 128 * p + 128] = rel[old, p, strided(0, 8), :].astype(BF)
        for j, rows in enumerate((slice(8, 16), slice(128, 136))):
            ends = [load(rel.at[old], rows, 4 * h) for h in range(2)]
            rs_[n, j] = jnp.concatenate(ends, axis=0).astype(BF)
        copies = []
        for j, (src, dst, dev) in enumerate((
            (ys.at[n, pl.ds(0, 16)], yr.at[n, pl.ds(0, 16)], ynext),
            (ys.at[n, pl.ds(16, 16)], yr.at[n, pl.ds(16, 16)], yprev),
            (rs_.at[n, 0], rr_.at[n, 0], above),
            (rs_.at[n, 1], rr_.at[n, 1], below),
        )):
            copy = pltpu.make_async_remote_copy(
                src_ref=src, dst_ref=dst, send_sem=it_ss.at[n, j], recv_sem=it_rs.at[n, j],
                device_id=dev, device_id_type=MESH,
            )
            copy.start()
            copies.append(copy)
        if last:
            for s in range(8):
                for p in range(8):
                    cols = slice(128 * (p % 4), 128 * (p % 4) + 128)
                    part = rel[old, p, strided(s, 8), :].astype(BF)
                    ret[0, p // 4, 16 * s : 16 * s + 16, cols] = part
            send_back(ret.at[0], early_ref, 0)

        def some(i4, _):
            for i in range(4):
                start = pl.multiple_of(i4 * 32, 32)
                rows = pl.ds(pl.multiple_of(start + 8 * i, 8), 8)
                mid = pl.ds(pl.multiple_of(start + 8 * i + 8, 8), 8)
                far = pl.ds(pl.multiple_of(start + 8 * i + 16, 8), 8)
                cs = [load(coef.at[k], rows) for k in range(7)]
                inner_n = jnp.where(sub == 7, 0.0, cs[4])
                inner_p = jnp.where(sub == 0, 0.0, cs[5])
                for h in range(2):
                    own = load(rel.at[old], mid, 4 * h)
                    acc = load(mf, rows, 4 * h) + cs[6] * own
                    acc += cs[0] * load(rel.at[old], far, 4 * h) + cs[1] * load(rel.at[old], rows, 4 * h)
                    acc += cs[2] * pltpu.roll(own, 511, 1) + cs[3] * pltpu.roll(own, 1, 1)
                    acc += inner_n * pltpu.roll(own, 7, 0) + inner_p * pltpu.roll(own, 1, 0)
                    store(rel.at[new], mid, acc, 4 * h)
            return 0

        lax.fori_loop(0, NODES // 4, some, 0)
        copies[2].wait()
        copies[3].wait()
        high = rr_[n, 1].astype(F32)
        low = rr_[n, 0].astype(F32)
        for p in range(8):
            part = slice(8 * (p // 4), 8 * (p // 4) + 8)
            cols = slice(128 * (p % 4), 128 * (p % 4) + 128)
            rel[new, p, 128:136] = rel[new, p, 128:136] + coef[0, p % 4, 120:128] * low[part, cols]
            rel[new, p, 8:16] = rel[new, p, 8:16] + coef[1, p % 4, 0:8] * high[part, cols]
        copies[0].wait()
        copies[1].wait()
        for p in range(8):
            cols = slice(128 * p, 128 * p + 128)
            edge = rel[new, p, strided(0, 8), :] + cp0[p] * yr[n, 0:16, cols].astype(F32)
            rel[new, p, strided(0, 8), :] = edge
            edge = rel[new, p, strided(7, 8), :] + cn7[p] * yr[n, 16:32, cols].astype(F32)
            rel[new, p, strided(7, 8), :] = edge

    def several(n, _):
        relax(n, False)
        return 0

    lax.fori_loop(0, ITERS - 2, several, 0)
    relax(ITERS - 2, True)

    done = (ITERS - 1) % 2
    for s in range(8):
        for p in range(8):
            cols = slice(128 * (p % 4), 128 * (p % 4) + 128)
            rows = slice(16 * s, 16 * s + 16)
            sent = ret[0, p // 4, rows, cols].astype(F32)
            ret[1, p // 4, rows, cols] = (rel[done, p, strided(s, 8), :] - sent).astype(BF)
    send_back(ret.at[1], late_ref, 1)
    for half, dst in enumerate((early_ref, late_ref)):
        for k in range(1, 8):
            oc = part_of((e + 8 - k) % 8, t)
            pltpu.make_async_remote_copy(
                src_ref=ret.at[half, :, pl.ds(0, 16)], dst_ref=dst.at[:, 0, pl.ds(pl.multiple_of(16 * oc, 16), 16)],
                send_sem=rt_ss.at[half, k], recv_sem=rt_rs.at[half, k], device_id=peers[k - 1], device_id_type=MESH,
            ).wait_recv()
    for copy in owns:
        copy.wait()
    for copy in returns + started + statics + sends:
        copy.wait_send()


def shards(images, offsets, springs, validity):
    dma = pltpu.SemaphoreType.DMA
    vm = pltpu.VMEM
    early, late = pl.pallas_call(
        kernel,
        out_shape=[jax.ShapeDtypeStruct((2, 1, 128, 512), BF)] * 2,
        in_specs=[pl.BlockSpec(memory_space=pltpu.HBM)] * 4,
        out_specs=[pl.BlockSpec(memory_space=pltpu.HBM)] * 2,
        scratch_shapes=[
            pltpu.SMEM((2, NOFF), jnp.int32),
            vm((512, 2048), BF),
            vm((2, 128, 512), jnp.int32),
            vm((128, 512), jnp.int32),
            vm((512, 2048), BF),
            vm((9, PIX, 2048), BF),
            vm((3, 128, 512), BF),
            vm((3, 9, NODES, 512), BF),
            vm((16, 512), BF),
            vm((16, 512), BF),
            vm((PIX * 16, 8, 128), F32),
            vm(((PIX + 2 * RAD) * SPAN, 8, 128), F32),
            vm((128, 2048), F32),
            vm((2, 48, 1024), BF),
            vm((2, 48, 1024), BF),
            vm((9, 4, 128, 128), F32),
            vm((8, 16, 128), F32),
            vm((8, 16, 128), F32),
            vm((8, 128, 128), F32),
            vm((16, 1024), F32),
            vm((16, 1024), F32),
            vm((2, 8, 144, 128), F32),
            vm((ITERS - 1, 32, 1024), BF),
            vm((ITERS - 1, 32, 1024), BF),
            vm((ITERS - 1, 2, 16, 512), BF),
            vm((ITERS - 1, 2, 16, 512), BF),
            vm((2, 2, 128, 512), BF),
            dma((4, 8)), dma((4, 8)), dma((4,)), dma((4,)), dma((8,)), dma((8,)), dma, dma,
            dma((2,)), dma((2,)), dma, dma, dma, dma,
            dma((ITERS - 1, 4)), dma((ITERS - 1, 4)), dma((2, 8)), dma((2, 8)), dma((8,)),
        ],
        compiler_params=pltpu.CompilerParams(
            collective_id=0, has_side_effects=True, vmem_limit_bytes=61 * 1024 * 1024
        ),
    )(offsets.T, images, springs, validity)
    return early.astype(F32) + late.astype(F32)


def solution(mesh):
    in_specs = (
        P("sec", "strip", None),
        P(),
        P(None, "sec", "strip", None),
        P("sec", "strip", None),
    )
    out_specs = P(None, "sec", "strip", None)
    return jax.shard_map(shards, mesh=mesh, in_specs=in_specs, out_specs=out_specs, check_vma=False)
```

```python
import jax
import jax.numpy as jnp
from jax import lax
from jax.experimental import pallas as pl
from jax.experimental.pallas import tpu as pltpu
from jax.sharding import PartitionSpec as P

RAD = 3
ITERS = 8
SHARPNESS = 0.5
RELAX_RATE = 0.8
NOFF = 25
LOG2_E = 1.4426950408889634

BF = jnp.bfloat16
F32 = jnp.float32
MESH = pl.DeviceIdType.MESH

GROUP = 8
PIX = 64
NODES = 16
SPAN = 40
ORDER = (0, 1, 3, 2)


def part_of(e, t):
    n = jnp.where(e < 4, e, 11 - e)
    return jnp.where(t % 2 == 0, n, 7 - n)


def member_of(c, t):
    n = jnp.where(t % 2 == 0, c, 7 - c)
    return jnp.where(n < 4, n, 11 - n)


def load(ref, rows, first=0):
    return jnp.concatenate([ref[first + q, rows, :] for q in range(4)], axis=1)


def store(ref, rows, value, first=0):
    for q in range(4):
        ref[first + q, rows, :] = value[:, 128 * q : 128 * q + 128]


def iota(shape, dim):
    return lax.broadcasted_iota(jnp.int32, shape, dim)


def kernel(
    off_hbm, x_hbm, sp_hbm, va_hbm, early_ref, late_ref,
    off_ref, x_ref, sp_ref, va_ref, xs, got, ws, wgot, wup_s, wup_r, cur, nxt, tmp, hs, hr, coef, cn7, cp0, mf, e0s, e0r, corner, step_s, step_n, step_e, delta, rel, ys, yr, rs_, rr_, ret,
    img_ss, img_rs, fwd_ss, fwd_rs, st_ss, st_rs, ms_ss, ms_rs, hl_ss, hl_rs, wu_ss, wu_rs, e0_ss, e0_rs,
    co_ss, co_rs, sp_ss, sp_rs, it_ss, it_rs, rt_ss, rt_rs, in_sem,
):
    sec = lax.axis_index("sec")
    t = lax.axis_index("strip")
    y, e = sec // 8, sec % 8
    c = part_of(e, t)
    g = t * 8 + c

    def row_device(h, group):
        h = (h + 32) % 32
        tt = h // 8
        return (8 * group + member_of(h % 8, tt), tt)

    peers = [(8 * y + (e + k) % 8, t) for k in range(1, 8)]
    ynext = ((sec + 8) % 32, t)
    yprev = ((sec + 24) % 32, t)
    below = row_device(g + 1, y)
    above = row_device(g - 1, y)
    later, former = (y + 1) % 4, (y + 3) % 4
    barrier = pltpu.get_barrier_semaphore()
    everyone = peers + [ynext, yprev, below, above]
    senders = [row_device(g + 1, former), row_device(g - 1, former)]
    for d in everyone + senders:
        pl.semaphore_signal(barrier, inc=1, device_id=d, device_id_type=MESH)

    chunks = []
    for i in range(4):
        rows = pl.ds(128 * i, 128)
        chunks.append(pltpu.make_async_copy(x_hbm.at[0, rows], x_ref.at[rows], in_sem.at[i]))
    others = [
        pltpu.make_async_copy(sp_hbm.at[:, 0], sp_ref, in_sem.at[4]),
        pltpu.make_async_copy(va_hbm.at[0], va_ref, in_sem.at[5]),
        pltpu.make_async_copy(off_hbm, off_ref, in_sem.at[6]),
    ]
    for copy in chunks + others:
        copy.start()

    source = iota((512, 512), 0)
    target = iota((512, 512), 1)
    spread = (source == 4 * (target % 128) + target // 128).astype(F32).astype(BF)

    for i in range(4):
        chunks[i].wait()
        rows = slice(128 * i, 128 * i + 128)
        for q in range(4):
            cols = slice(512 * q, 512 * q + 512)
            xs[rows, cols] = jnp.dot(x_ref[rows, cols], spread, preferred_element_type=F32).astype(BF)
    for copy in others:
        copy.wait()

    row_ids = iota((128, 512), 0)
    col_ids = iota((128, 512), 1)
    last_strip = lax.axis_size("strip") - 1
    wr_own = jnp.where((row_ids == 127) & (t == last_strip), 0.0, 0.25 * sp_ref[0].astype(F32))
    wc_own = jnp.where(col_ids == 511, 0.0, 0.25 * sp_ref[1].astype(F32))
    m_own = jnp.where(sec == lax.axis_size("sec") - 1, 0.0, va_ref[...].astype(F32))
    ws[0] = wr_own.astype(BF)
    ws[1] = m_own.astype(BF)
    ws[2] = wc_own.astype(BF)

    a = iota((128, 128), 0)
    b = iota((128, 128), 1)
    turn = (b == (a % 8) * 16 + a // 8).astype(F32).astype(BF)

    pl.semaphore_wait(barrier, len(everyone) + len(senders))

    sends = []

    def remote(src, dst, ss, rs, dev):
        copy = pltpu.make_async_remote_copy(
            src_ref=src, dst_ref=dst, send_sem=ss, recv_sem=rs, device_id=dev, device_id_type=MESH
        )
        copy.start()
        sends.append(copy)
        return copy

    def image_copy(blk, k):
        other = (e + k) % 8
        oc = part_of(other, t)
        src = xs.at[pl.ds(pl.multiple_of(64 * oc + 16 * blk, 16), 16)]
        return pltpu.make_async_remote_copy(
            src_ref=src, dst_ref=got.at[e, pl.ds(16 * blk, 16)], send_sem=img_ss.at[blk, k],
            recv_sem=img_rs.at[blk, e], device_id=peers[k - 1], device_id_type=MESH,
        )

    def image_from(blk, s):
        return pltpu.make_async_remote_copy(
            src_ref=xs.at[pl.ds(0, 16)], dst_ref=got.at[s, pl.ds(16 * blk, 16)], send_sem=img_ss.at[blk, 0],
            recv_sem=img_rs.at[blk, s], device_id=peers[0], device_id_type=MESH,
        )

    def static_copy(k, part):
        own = pl.ds(0, 2) if part == 0 else pl.ds(2, 1)
        other = (e + k) % 8
        oc = part_of(other, t)
        return pltpu.make_async_remote_copy(
            src_ref=ws.at[own, pl.ds(pl.multiple_of(16 * oc, 16), 16)], dst_ref=wgot.at[own, e + 1],
            send_sem=st_ss.at[part, k], recv_sem=st_rs.at[part, k], device_id=peers[k - 1], device_id_type=MESH,
        )

    started = []
    for blk in ORDER:
        for k in range(1, 8):
            copy = image_copy(blk, k)
            copy.start()
            started.append(copy)
    statics_a = [static_copy(k, 0) for k in range(1, 8)]
    statics_b = [static_copy(k, 1) for k in range(1, 8)]
    statics = statics_a + statics_b
    got[e] = xs[pl.ds(pl.multiple_of(64 * c, 64), 64)]
    wgot[:, e + 1] = ws[:, pl.ds(pl.multiple_of(16 * c, 16), 16)]

    def forward(blk):
        @pl.when(e != 0)
        def _():
            image_from(blk, 0).wait_recv()

        return remote(got.at[0, pl.ds(16 * blk, 16)], got.at[8, pl.ds(16 * blk, 16)],
                      fwd_ss.at[blk], fwd_rs.at[blk], yprev)

    def arrive(blk):
        for s in range(1, 8):
            @pl.when(e != s)
            def _():
                image_from(blk, s).wait_recv()

    lane = iota((8, 128), 1)

    def expand(row, src_row):
        base = (row + RAD) * SPAN
        right, left = {}, {}
        for q in range(4):
            for w in range(4):
                plane = tmp[pl.ds(src_row, 8), 512 * q + 128 * w : 512 * q + 128 * w + 128]
                nxt[base + 10 * q + w + 3] = plane
                if w > 0:
                    right[q, w] = pltpu.roll(plane, 1, 1)
                if w < 3:
                    left[q, w] = pltpu.roll(plane, 127, 1)
        for q in range(4):
            for w in range(1, 4):
                carry = right[q - 1, w] if q else jnp.zeros((8, 128), F32)
                nxt[base + 10 * q + w - 1] = jnp.where(lane == 0, carry, right[q, w])
            for w in range(3):
                carry = left[q + 1, w] if q < 3 else jnp.zeros((8, 128), F32)
                nxt[base + 10 * q + w + 7] = jnp.where(lane == 127, carry, left[q, w])

    def convert_own(blk):
        rows = slice(16 * blk, 16 * blk + 16)
        here = jnp.dot(turn, got[0:8, rows].reshape(128, 2048), preferred_element_type=F32)
        for r in range(16):
            for p in range(16):
                cur[(16 * blk + r) * 16 + p] = here[8 * r : 8 * r + 8, 128 * p : 128 * p + 128]

    def convert(blk):
        rows = slice(16 * blk, 16 * blk + 16)
        tmp[...] = jnp.dot(turn, got[1:9, rows].reshape(128, 2048), preferred_element_type=F32)

        def one(r, _):
            expand(16 * blk + r, pl.multiple_of(r * 8, 8))
            return 0

        lax.fori_loop(0, 16, one, 0)

    def score(first, count):
        def one(i, _):
            q4 = i % 4
            row = first + i // 4
            mine = [[cur[((4 * row + q) * 4 + q4) * 4 + w] for w in range(4)] for q in range(4)]
            scores = []
            for k in range(NOFF):
                at = (4 * row + off_ref[0, k] + RAD) * SPAN + 10 * q4 + off_ref[1, k] + RAD
                parts = []
                for q in range(4):
                    p = [mine[q][w] * nxt[at + (q * SPAN + w)] for w in range(4)]
                    parts.append((p[0] + p[1]) + (p[2] + p[3]))
                scores.append((parts[0] + parts[1]) + (parts[2] + parts[3]))
            top = scores[0]
            for k in range(1, NOFF):
                top = jnp.maximum(top, scores[k])
            total = jnp.zeros((8, 128), F32)
            down = jnp.zeros((8, 128), F32)
            side = jnp.zeros((8, 128), F32)
            for k in range(NOFF):
                soft = jnp.exp2((SHARPNESS * LOG2_E) * (scores[k] - top))
                total += soft
                down += soft * off_ref[0, k].astype(F32)
                side += soft * off_ref[1, k].astype(F32)
            rows = pl.ds(pl.multiple_of(row * 8, 8), 8)
            scale = 1.0 / total
            mf[q4, rows] = down * scale
            mf[4 + q4, rows] = side * scale
            return 0

        lax.fori_loop(0, 4 * count, one, 0, unroll=2)

    def halves(rows):
        return jnp.concatenate([tmp[rows, 0:1024], tmp[rows, 1024:2048]], axis=0).astype(BF)

    def halo(j, row, outside):
        came = jnp.where(outside, 0.0, hr[j].astype(F32))
        tmp[0:24, 0:1024] = came[0:24]
        tmp[0:24, 1024:2048] = came[24:48]

        def one(r, _):
            expand(row + r, pl.multiple_of(r * 8, 8))
            return 0

        lax.fori_loop(0, 3, one, 0)

    every = slice(0, 128)
    forward_0 = forward(0)
    arrive(0)
    convert_own(0)
    forward_0.wait_recv()
    convert(0)
    hs[0] = halves(slice(0, 24))
    forward_1 = forward(1)
    arrive(1)
    convert_own(1)
    forward_1.wait_recv()
    convert(1)
    forward_3 = forward(3)
    score(1, 4)
    arrive(3)
    convert_own(3)
    for copy in statics:
        copy.start()
    forward_3.wait_recv()
    convert(3)
    hs[1] = halves(slice(104, 128))
    forward_2 = forward(2)
    halo_up = remote(hs.at[0], hr.at[1], hl_ss.at[0], hl_rs.at[0], above)
    halo_down = remote(hs.at[1], hr.at[0], hl_ss.at[1], hl_rs.at[1], below)
    score(5, 2)
    arrive(2)
    convert_own(2)
    score(13, 2)

    for copy in statics_a:
        copy.wait_recv()
    match_copy = remote(wgot.at[1, 8], wgot.at[1, 0], ms_ss, ms_rs, ynext)
    wr = jnp.dot(turn, wgot[0, 1:9].reshape(128, 512), preferred_element_type=F32)
    wup_s[...] = jnp.concatenate([wr[120:128], wr[120:128]], axis=0).astype(BF)
    up_copy = remote(wup_s, wup_r, wu_ss, wu_rs, below)
    store(coef.at[0], every, wr)
    store(coef.at[8], every, jnp.dot(turn, wgot[1, 1:9].reshape(128, 512), preferred_element_type=F32))
    forward_2.wait_recv()
    convert(2)
    score(7, 6)
    for copy in statics_b:
        copy.wait_recv()
    store(coef.at[2], every, jnp.dot(turn, wgot[2, 1:9].reshape(128, 512), preferred_element_type=F32))

    match_copy.wait_recv()
    up_copy.wait_recv()
    store(coef.at[5], every, jnp.dot(turn, wgot[1, 0:8].reshape(128, 512), preferred_element_type=F32))
    sub = iota((8, 512), 0)
    col = iota((8, 512), 1)
    for p in range(8):
        for o in range(2):
            rel[o, p, 0:8] = jnp.zeros((8, 128), F32)
            rel[o, p, 136:144] = jnp.zeros((8, 128), F32)
    wu_next = wup_r[...].astype(F32)[0:8]
    for i in range(NODES):
        rows = slice(8 * i, 8 * i + 8)
        wu = wu_next
        wr = load(coef.at[0], rows)
        wu_next = wr
        wc = load(coef.at[2], rows)
        m = load(coef.at[8], rows)
        mp = load(coef.at[5], rows)
        wl = jnp.where(col == 0, 0.0, pltpu.roll(wc, 1, 1))
        diagonal = wr + wu + wc + wl + m + mp
        step = RELAX_RATE / (1.0 + diagonal)
        for k, factor in enumerate((wr, wu, wc, wl, m, mp)):
            store(coef.at[k], rows, step * factor)
        store(coef.at[6], rows, 1.0 - step * diagonal)
        store(coef.at[7], rows, step)

    def strided(s, start=0):
        return pl.ds(start + s, NODES, stride=8)

    for p in range(8):
        cn7[p] = coef[4, p % 4, strided(7), :]
        cp0[p] = coef[5, p % 4, strided(0), :]
        delta[p] = jnp.zeros((32, 128), F32)
    for p in range(4):
        step_s[p] = coef[7, p, strided(0), :]
    steps = [
        remote(step_s, step_n, sp_ss.at[0], sp_rs.at[0], yprev),
        remote(coef.at[7, :, pl.ds(0, 8)], step_e.at[1], sp_ss.at[1], sp_rs.at[1], above),
        remote(coef.at[7, :, pl.ds(120, 8)], step_e.at[0], sp_ss.at[2], sp_rs.at[2], below),
    ]

    halo_up.wait_recv()
    halo(1, PIX, g == 31)
    halo_down.wait_recv()
    halo(0, -RAD, g == 0)
    score(0, 1)
    score(15, 1)

    for p in range(8):
        e0s[:, 128 * p : 128 * p + 128] = mf[p, strided(7), :] * coef[8, p % 4, strided(7), :]
    e0 = remote(e0s, e0r, e0_ss, e0_rs, ynext)
    corners = [
        remote(e0s.at[pl.ds(8, 8)], corner.at[0], co_ss.at[0], co_rs.at[0], row_device(g + 1, later)),
        remote(e0s.at[pl.ds(0, 8)], corner.at[1], co_ss.at[1], co_rs.at[1], row_device(g - 1, later)),
    ]
    for i in range(NODES):
        rows = slice(8 * i, 8 * i + 8)
        m = load(coef.at[8], rows)
        step = load(coef.at[7], rows)
        for h in range(2):
            own = m * load(mf, rows, 4 * h)
            pushed = step * (jnp.where(sub == 0, 0.0, pltpu.roll(own, 1, 0)) - own)
            store(mf, rows, pushed, 4 * h)
            store(rel.at[0], slice(8 * i + 8, 8 * i + 16), pushed, 4 * h)

    def missing(new):
        e0.wait_recv()
        for p in range(8):
            delta[p, 8:24] = coef[7, p % 4, strided(0), :] * e0r[:, 128 * p : 128 * p + 128]
        for h in range(2):
            own = load(delta, slice(8, 24), 4 * h)

            def factor(k, s):
                return jnp.concatenate([coef[k, q, strided(s), :] for q in range(4)], axis=1)

            acc = own + factor(6, 0) * own
            acc += factor(0, 0) * load(delta, slice(9, 25), 4 * h) + factor(1, 0) * load(delta, slice(7, 23), 4 * h)
            acc += factor(2, 0) * pltpu.roll(own, 511, 1) + factor(3, 0) * pltpu.roll(own, 1, 1)
            aside = factor(5, 1) * own
            for q in range(4):
                p = 4 * h + q
                cols = slice(128 * q, 128 * q + 128)
                rel[new, p, strided(0, 8), :] = rel[new, p, strided(0, 8), :] + acc[:, cols]
                rel[new, p, strided(1, 8), :] = rel[new, p, strided(1, 8), :] + aside[:, cols]
                mf[p, strided(0), :] = mf[p, strided(0), :] + own[:, cols]

    def send_back(src, dst, half):
        for k in range(1, 8):
            other = (e + k) % 8
            copy = pltpu.make_async_remote_copy(
                src_ref=src.at[:, pl.ds(pl.multiple_of(16 * other, 16), 16)], dst_ref=dst.at[:, 0, place],
                send_sem=rt_ss.at[half, k], recv_sem=rt_rs.at[half, k], device_id=peers[k - 1], device_id_type=MESH,
            )
            copy.start()
            returns.append(copy)
        own = pltpu.make_async_copy(
            src.at[:, pl.ds(pl.multiple_of(16 * e, 16), 16)], dst.at[:, 0, place], rt_ss.at[half, 0]
        )
        own.start()
        owns.append(own)

    returns, owns = [], []
    place = pl.ds(pl.multiple_of(16 * c, 16), 16)

    def relax(n, first, last):
        old = n % 2
        new = 1 - old
        for p in range(8):
            ys[n, 0:16, 128 * p : 128 * p + 128] = rel[old, p, strided(7, 8), :].astype(BF)
            ys[n, 16:32, 128 * p : 128 * p + 128] = rel[old, p, strided(0, 8), :].astype(BF)
        for j, rows in enumerate((slice(8, 16), slice(128, 136))):
            ends = [load(rel.at[old], rows, 4 * h) for h in range(2)]
            rs_[n, j] = jnp.concatenate(ends, axis=0).astype(BF)
        copies = []
        for j, (src, dst, dev) in enumerate((
            (ys.at[n, pl.ds(0, 16)], yr.at[n, pl.ds(0, 16)], ynext),
            (ys.at[n, pl.ds(16, 16)], yr.at[n, pl.ds(16, 16)], yprev),
            (rs_.at[n, 0], rr_.at[n, 0], above),
            (rs_.at[n, 1], rr_.at[n, 1], below),
        )):
            copy = pltpu.make_async_remote_copy(
                src_ref=src, dst_ref=dst, send_sem=it_ss.at[n, j], recv_sem=it_rs.at[n, j],
                device_id=dev, device_id_type=MESH,
            )
            copy.start()
            copies.append(copy)
        if last:
            for s in range(8):
                for p in range(8):
                    cols = slice(128 * (p % 4), 128 * (p % 4) + 128)
                    part = rel[old, p, strided(s, 8), :].astype(BF)
                    ret[0, p // 4, 16 * s : 16 * s + 16, cols] = part
            send_back(ret.at[0], early_ref, 0)

        def some(i4, _):
            for i in range(4):
                start = pl.multiple_of(i4 * 32, 32)
                rows = pl.ds(pl.multiple_of(start + 8 * i, 8), 8)
                mid = pl.ds(pl.multiple_of(start + 8 * i + 8, 8), 8)
                far = pl.ds(pl.multiple_of(start + 8 * i + 16, 8), 8)
                cs = [load(coef.at[k], rows) for k in range(7)]
                inner_n = jnp.where(sub == 7, 0.0, cs[4])
                inner_p = jnp.where(sub == 0, 0.0, cs[5])
                for h in range(2):
                    own = load(rel.at[old], mid, 4 * h)
                    acc = load(mf, rows, 4 * h) + cs[6] * own
                    acc += cs[0] * load(rel.at[old], far, 4 * h) + cs[1] * load(rel.at[old], rows, 4 * h)
                    acc += cs[2] * pltpu.roll(own, 511, 1) + cs[3] * pltpu.roll(own, 1, 1)
                    acc += inner_n * pltpu.roll(own, 7, 0) + inner_p * pltpu.roll(own, 1, 0)
                    store(rel.at[new], mid, acc, 4 * h)
            return 0

        lax.fori_loop(0, NODES // 4, some, 0)
        if first:
            missing(new)
            for copy in corners + steps:
                copy.wait_recv()
        copies[2].wait()
        copies[3].wait()
        high = rr_[n, 1].astype(F32)
        low = rr_[n, 0].astype(F32)
        for p in range(8):
            part = slice(8 * (p // 4), 8 * (p // 4) + 8)
            cols = slice(128 * (p % 4), 128 * (p % 4) + 128)
            over, under = high[part, cols], low[part, cols]
            if first:
                at = slice(128 * p, 128 * p + 128)
                over += jnp.where(sub[:, 0:128] == 0, step_e[0, p % 4] * corner[0, 7:8, at], 0.0)
                under += jnp.where(sub[:, 0:128] == 0, step_e[1, p % 4] * corner[1, 0:1, at], 0.0)
            rel[new, p, 128:136] = rel[new, p, 128:136] + coef[0, p % 4, 120:128] * under
            rel[new, p, 8:16] = rel[new, p, 8:16] + coef[1, p % 4, 0:8] * over
        copies[0].wait()
        copies[1].wait()
        for p in range(8):
            cols = slice(128 * p, 128 * p + 128)
            edge = rel[new, p, strided(0, 8), :] + cp0[p] * yr[n, 0:16, cols].astype(F32)
            rel[new, p, strided(0, 8), :] = edge
            after = yr[n, 16:32, cols].astype(F32)
            if first:
                after += step_n[p % 4] * e0s[:, cols]
            edge = rel[new, p, strided(7, 8), :] + cn7[p] * after
            rel[new, p, strided(7, 8), :] = edge

    def several(n, _):
        relax(n, False, False)
        return 0

    relax(0, True, False)
    lax.fori_loop(1, ITERS - 2, several, 0)
    relax(ITERS - 2, False, True)

    done = (ITERS - 1) % 2
    for s in range(8):
        for p in range(8):
            cols = slice(128 * (p % 4), 128 * (p % 4) + 128)
            rows = slice(16 * s, 16 * s + 16)
            sent = ret[0, p // 4, rows, cols].astype(F32)
            ret[1, p // 4, rows, cols] = (rel[done, p, strided(s, 8), :] - sent).astype(BF)
    send_back(ret.at[1], late_ref, 1)
    for half, dst in enumerate((early_ref, late_ref)):
        for k in range(1, 8):
            oc = part_of((e + 8 - k) % 8, t)
            pltpu.make_async_remote_copy(
                src_ref=ret.at[half, :, pl.ds(0, 16)], dst_ref=dst.at[:, 0, pl.ds(pl.multiple_of(16 * oc, 16), 16)],
                send_sem=rt_ss.at[half, k], recv_sem=rt_rs.at[half, k], device_id=peers[k - 1], device_id_type=MESH,
            ).wait_recv()
    for copy in owns:
        copy.wait()
    for copy in returns + started + statics + sends:
        copy.wait_send()


def shards(images, offsets, springs, validity):
    dma = pltpu.SemaphoreType.DMA
    vm = pltpu.VMEM
    early, late = pl.pallas_call(
        kernel,
        out_shape=[jax.ShapeDtypeStruct((2, 1, 128, 512), BF)] * 2,
        in_specs=[pl.BlockSpec(memory_space=pltpu.HBM)] * 4,
        out_specs=[pl.BlockSpec(memory_space=pltpu.HBM)] * 2,
        scratch_shapes=[
            pltpu.SMEM((2, NOFF), jnp.int32),
            vm((512, 2048), BF),
            vm((2, 128, 512), jnp.int32),
            vm((128, 512), jnp.int32),
            vm((512, 2048), BF),
            vm((9, PIX, 2048), BF),
            vm((3, 128, 512), BF),
            vm((3, 9, NODES, 512), BF),
            vm((16, 512), BF),
            vm((16, 512), BF),
            vm((PIX * 16, 8, 128), F32),
            vm(((PIX + 2 * RAD) * SPAN, 8, 128), F32),
            vm((128, 2048), F32),
            vm((2, 48, 1024), BF),
            vm((2, 48, 1024), BF),
            vm((9, 4, 128, 128), F32),
            vm((8, 16, 128), F32),
            vm((8, 16, 128), F32),
            vm((8, 128, 128), F32),
            vm((16, 1024), F32),
            vm((16, 1024), F32),
            vm((2, 8, 1024), F32),
            vm((4, 16, 128), F32),
            vm((4, 16, 128), F32),
            vm((2, 4, 8, 128), F32),
            vm((8, 32, 128), F32),
            vm((2, 8, 144, 128), F32),
            vm((ITERS - 1, 32, 1024), BF),
            vm((ITERS - 1, 32, 1024), BF),
            vm((ITERS - 1, 2, 16, 512), BF),
            vm((ITERS - 1, 2, 16, 512), BF),
            vm((2, 2, 128, 512), BF),
            dma((4, 8)), dma((4, 8)), dma((4,)), dma((4,)), dma((2, 8)), dma((2, 8)), dma, dma,
            dma((2,)), dma((2,)), dma, dma, dma, dma,
            dma((2,)), dma((2,)), dma((3,)), dma((3,)),
            dma((ITERS - 1, 4)), dma((ITERS - 1, 4)), dma((2, 8)), dma((2, 8)), dma((8,)),
        ],
        compiler_params=pltpu.CompilerParams(
            collective_id=0, has_side_effects=True, vmem_limit_bytes=61 * 1024 * 1024
        ),
    )(offsets.T, images, springs, validity)
    return early.astype(F32) + late.astype(F32)


def solution(mesh):
    in_specs = (
        P("sec", "strip", None),
        P(),
        P(None, "sec", "strip", None),
        P("sec", "strip", None),
    )
    out_specs = P(None, "sec", "strip", None)
    return jax.shard_map(shards, mesh=mesh, in_specs=in_specs, out_specs=out_specs, check_vma=False)
```
